32 devices in a mesh: groups: 2 (over x), grid: 16 (over z, y, core).
Axes of the slice: x: 2, y: 2, z: 4, core: 2. Of those that a mesh axis runs over, the one named last changes fastest.
Arguments:
- source: bfloat16 [1536, 8192], P('groups', 'grid'), parts along dimension 0, may hold values from -6 to 6
- target: bfloat16 [1536, 8192], P('groups', 'grid'), parts along dimension 0, may hold values from -6 to 6
Outputs:
- cross_gram: float32 [16384, 8192], P(('groups', 'grid')), parts along dimension 0
- self_gram: float32 [16384, 8192], P(('groups', 'grid')), parts along dimension 0
The draws below stay inside these ranges and needn't reach their ends.
There are 2 independent parts, one for each index of `groups`. The reference program is written for one: setup_inputs(seed, part) draws one part's arguments, and reference() takes and returns one part's arrays. A program takes and returns all parts, laid end to end along the dimension named above; each array names one. Nothing has to cross between parts.
All inputs are finite; a program needn't handle non-finite values.
Results may differ from the reference program's by a relative error of at most 0.0003.
Values may be sent and summed in bfloat16 or wider, within the bound.
A program may use at most 128 MiB of HBM per device.

```python
import jax
import jax.numpy as jnp

D = 8192
TOKENS = 768


def level_of(stream_key, shape, pieces, least, top_value):
    def one(axis_at, shards_of):
        draws = jax.random.uniform(jax.random.fold_in(jax.random.fold_in(stream_key, 6), axis_at), (shards_of,), jnp.float32, least / len(pieces), top_value / len(pieces))
        return jnp.repeat(jnp.exp(draws), shape[axis_at] // shards_of).reshape((-1,) + (1,) * (len(shape) - axis_at - 1))

    level = one(*pieces[0])
    for cut in pieces[1:]:
        level = level * one(*cut)
    return level


def noise(rng, dims, scale, most, pieces=(), held_as=jnp.bfloat16):
    drawn = scale * jax.random.normal(rng, dims, jnp.float32)
    if pieces:
        drawn = drawn * level_of(rng, dims, pieces, -0.22, 0.18)
    return jnp.clip(drawn, -most, most).astype(held_as)


def setup_inputs(seed: int = 0, part: int = 0) -> dict:
    arg_keys = jax.random.split(jax.random.key(seed), 3)
    own_keys = jax.random.split(jax.random.fold_in(arg_keys[2], part), 3)
    source = noise(own_keys[0], (TOKENS, D), 1.0, 6.0, ((1, 16),))
    target = noise(own_keys[1], (TOKENS, D), 1.0, 6.0, ((1, 16),))
    return {"source": source, "target": target}


def reference(source, target):
    cross = jnp.dot(source.T, target, preferred_element_type=jnp.float32)
    selfg = jnp.dot(source.T, source, preferred_element_type=jnp.float32)
    return cross / TOKENS, selfg / TOKENS
```

```python
import functools

import jax
import jax.numpy as jnp
from jax import lax
from jax.experimental import pallas as pl
from jax.experimental.pallas import tpu as pltpu
from jax.sharding import PartitionSpec as P

MESH = pl.DeviceIdType.MESH


def gather_kernel(Z, Y, PA, PB, s_ref, t_ref, g, local_sem, recv, crecv, zsend, zsendp, ysend, csend):
    K = PA + PB
    tokens, width = s_ref.shape
    R = 2 * tokens // K
    me = lax.axis_index("grid")
    c = me % 2
    y = (me // 2) % Y
    z = me // (2 * Y)

    def dev(zz, yy, cc):
        return (zz * Y + yy) * 2 + cc

    def rows(p):
        return pl.ds(pl.multiple_of(p * R, R), R)

    left, right = dev(z - 1, y, c), dev(z + 1, y, c)
    partner, sibling = dev(z, Y - 1 - y, c), dev(z, y, 1 - c)
    has_left, has_right = z > 0, z < Z - 1

    barrier = pltpu.get_barrier_semaphore()

    def greet(target):
        pl.semaphore_signal(barrier, inc=1, device_id={"grid": target}, device_id_type=MESH)

    @pl.when(has_left)
    def _():
        greet(left)

    @pl.when(has_right)
    def _():
        greet(right)

    if Y > 1:
        greet(partner)
    greet(sibling)
    pl.semaphore_wait(
        barrier, (2 if Y > 1 else 1) + has_left.astype(jnp.int32) + has_right.astype(jnp.int32)
    )

    def remote(src, dst, send, got, target):
        return pltpu.make_async_remote_copy(
            src_ref=src, dst_ref=dst, send_sem=send, recv_sem=got,
            device_id={"grid": target}, device_id_type=MESH,
        )

    def own(p):
        half = K // 2
        ref = s_ref if p < half else t_ref
        return ref.at[pl.ds((p % half) * R, R), :]

    order = list(range(PA, K)) + list(range(PA))
    if Y > 1:
        for p in order:
            remote(own(p), g.at[me, pl.ds(p * R, R), :], ysend.at[z], recv.at[z * Y + y, p], partner).start()

    @pl.when(has_right)
    def _():
        for p in range(K):
            remote(own(p), g.at[me, pl.ds(p * R, R), :], zsend.at[0, z], recv.at[z * Y + y, p], right).start()

    @pl.when(has_left)
    def _():
        for p in range(K):
            remote(own(p), g.at[me, pl.ds(p * R, R), :], zsend.at[1, z], recv.at[z * Y + y, p], left).start()

    locals_ = []
    for h, ref in enumerate((s_ref, t_ref)):
        dst = g.at[me, pl.ds(h * tokens, tokens), :]
        remote(ref, dst, csend.at[z * Y + y], crecv.at[z * Y + y], sibling).start()
        cp = pltpu.make_async_copy(ref, dst, local_sem.at[h])
        cp.start()
        locals_.append(cp)

    def wait_piece(zz, yy, p):
        at = g.at[dev(zz, yy, c), rows(p), :]
        remote(at, at, csend.at[zz * Y + yy], recv.at[zz * Y + yy, p], sibling).wait_recv()

    def send_piece(zz, yy, p, send, target):
        at = g.at[dev(zz, yy, c), rows(p), :]
        remote(at, at, send, recv.at[zz * Y + yy, p], target).start()

    def share_piece(zz, yy, p):
        at = g.at[dev(zz, yy, c), rows(p), :]
        remote(at, at, csend.at[zz * Y + yy], crecv.at[zz * Y + yy], sibling).start()

    per = K + (PB if Y > 1 else 0)
    n_left, n_right = z, Z - 1 - z
    least = jnp.minimum(n_left, n_right)

    def from_z(t, side):
        k = t // per + 1
        q = t % per
        zo = z - k if side == 0 else z + k
        there = zo >= 0 if side == 0 else zo <= Z - 1
        onward = has_right if side == 0 else has_left
        target = right if side == 0 else left

        @pl.when(there & (q < K))
        def _():
            wait_piece(zo, y, q)

            @pl.when(onward)
            def _():
                send_piece(zo, y, q, zsend.at[side, zo], target)

            if Y > 1:
                @pl.when(q < PA)
                def _():
                    send_piece(zo, y, q, ysend.at[zo], partner)

            share_piece(zo, y, q)

        if Y > 1 and PB > 0:
            @pl.when(there & (q >= K))
            def _():
                yo, p = Y - 1 - y, q - PB
                wait_piece(zo, yo, p)

                @pl.when(onward)
                def _():
                    send_piece(zo, yo, p, zsendp.at[side, zo], target)

                share_piece(zo, yo, p)

    def from_y(u):
        yo = Y - 1 - y

        @pl.when(u < PB)
        def _():
            p = PA + u
            wait_piece(z, yo, p)

            @pl.when(has_right)
            def _():
                send_piece(z, yo, p, zsendp.at[0, z], right)

            @pl.when(has_left)
            def _():
                send_piece(z, yo, p, zsendp.at[1, z], left)

            share_piece(z, yo, p)

        @pl.when((u >= PB) & (u < K))
        def _():
            p = u - PB
            wait_piece(z, yo, p)
            share_piece(z, yo, p)

        @pl.when(u >= K)
        def _():
            i = u - K
            both = i < 2 * PA * least
            i1 = i - 2 * PA * least
            pair = i // 2
            k = jnp.where(both, pair // PA, least + i1 // PA) + 1
            p = jnp.where(both, pair % PA, i1 % PA)
            go_left = jnp.where(both, i % 2, (n_left < n_right).astype(jnp.int32))
            zo = jnp.where(go_left == 1, z + k, z - k)
            wait_piece(zo, yo, p)
            share_piece(zo, yo, p)

    slots = per * (Z - 1)
    y_slots = K + PA * (Z - 1) if Y > 1 else 0

    @pl.loop(0, max(slots, y_slots))
    def _(t):
        if y_slots:
            @pl.when(t < y_slots)
            def _():
                from_y(t)
        from_z(t, 0)
        from_z(t, 1)

    for cp in locals_:
        cp.wait()

    @pl.loop(0, Z)
    def _(zo):
        for side in range(2):
            sent = (zo <= z) & has_right if side == 0 else (zo >= z) & has_left

            @pl.when(sent)
            def _():
                at = g.at[0]
                remote(at, at, zsend.at[side, zo], crecv.at[0], sibling).wait_send()
                if Y > 1 and PB > 0:
                    at = g.at[0, pl.ds(PA * R, PB * R), :]
                    remote(at, at, zsendp.at[side, zo], crecv.at[0], sibling).wait_send()

        if Y > 1:
            @pl.when(zo == z)
            def _():
                at = g.at[0]
                remote(at, at, ysend.at[zo], crecv.at[0], sibling).wait_send()

            @pl.when(zo != z)
            def _():
                at = g.at[0, pl.ds(0, PA * R), :]
                remote(at, at, ysend.at[zo], crecv.at[0], sibling).wait_send()

        for yo in range(Y):
            at = g.at[dev(zo, yo, 1 - c)]
            remote(at, at, csend.at[zo * Y + yo], crecv.at[zo * Y + yo], sibling).wait()


def gather(source, target, Z, Y):
    tokens, width = source.shape
    PA, PB = (10, 2) if Y > 1 else (4, 0)
    n = Z * Y * 2
    dma = pltpu.SemaphoreType.DMA
    return pl.pallas_call(
        functools.partial(gather_kernel, Z, Y, PA, PB),
        out_shape=jax.ShapeDtypeStruct((n, 2 * tokens, width), source.dtype),
        in_specs=[pl.BlockSpec(memory_space=pl.ANY)] * 2,
        out_specs=pl.BlockSpec(memory_space=pl.ANY),
        scratch_shapes=[
            dma((2,)),
            dma((Z * Y, PA + PB)),
            dma((Z * Y,)),
            dma((2, Z)),
            dma((2, Z)),
            dma((Z,)),
            dma((Z * Y,)),
        ],
        compiler_params=pltpu.CompilerParams(collective_id=0, has_side_effects=True),
    )(source, target)


def product_kernel(scale, s_ref, g_ref, cross_ref, self_ref, st):
    tokens, width = s_ref.shape
    per = g_ref.shape[0]

    @pl.when(pl.program_id(0) == 0)
    def _():
        st[...] = s_ref[...].T

    for j in range(per):
        at = slice(j * width, (j + 1) * width)
        self_ref[:, at] = jnp.dot(st[...], g_ref[j, :tokens, :], preferred_element_type=jnp.float32) * scale
        cross_ref[:, at] = jnp.dot(st[...], g_ref[j, tokens:, :], preferred_element_type=jnp.float32) * scale


def products(source, gathered):
    tokens, width = source.shape
    n = gathered.shape[0]
    per = max(1, 512 // width)
    out = jax.ShapeDtypeStruct((width, n * width), jnp.float32)
    out_spec = pl.BlockSpec((width, per * width), lambda i: (0, i))
    return pl.pallas_call(
        functools.partial(product_kernel, 1.0 / tokens),
        grid=(n // per,),
        out_shape=(out, out),
        in_specs=[
            pl.BlockSpec((tokens, width), lambda i: (0, 0)),
            pl.BlockSpec((per, 2 * tokens, width), lambda i: (i, 0, 0)),
        ],
        out_specs=(out_spec, out_spec),
        scratch_shapes=[pltpu.VMEM((width, tokens), source.dtype)],
        compiler_params=pltpu.CompilerParams(
            dimension_semantics=("arbitrary",), vmem_limit_bytes=32 << 20
        ),
        cost_estimate=pl.CostEstimate(
            flops=4 * width * width * n * tokens,
            bytes_accessed=n * width * (4 * tokens + 8 * width),
            transcendentals=0,
        ),
    )(source, gathered)


def solution(mesh):
    n = mesh.shape["grid"]
    Y = max(1, 4 // mesh.shape["groups"])
    Z = n // (2 * Y)

    def shards(source, target):
        gathered = gather(source, target, Z, Y)
        return products(source, gathered)

    specs = (P("groups", "grid"), P("groups", "grid"))
    out_specs = (P(("groups", "grid"), None), P(("groups", "grid"), None))
    return jax.shard_map(shards, mesh=mesh, in_specs=specs, out_specs=out_specs, check_vma=False)
```

```python
import functools

import jax
import jax.numpy as jnp
from jax import lax
from jax.experimental import pallas as pl
from jax.experimental.pallas import tpu as pltpu
from jax.sharding import PartitionSpec as P

MESH = pl.DeviceIdType.MESH


def gather_kernel(Z, Y, PA, PB, s_ref, t_ref, out, g, st, local_sem, recv, crecv, zsend, zsendp, ysend, csend):
    K = PA + PB
    tokens, width = s_ref.shape
    R = 2 * tokens // K
    me = lax.axis_index("grid")
    c = me % 2
    y = (me // 2) % Y
    z = me // (2 * Y)

    def dev(zz, yy, cc):
        return (zz * Y + yy) * 2 + cc

    def rows(p):
        return pl.ds(pl.multiple_of(p * R, R), R)

    left, right = dev(z - 1, y, c), dev(z + 1, y, c)
    partner, sibling = dev(z, Y - 1 - y, c), dev(z, y, 1 - c)
    has_left, has_right = z > 0, z < Z - 1

    barrier = pltpu.get_barrier_semaphore()

    def greet(target):
        pl.semaphore_signal(barrier, inc=1, device_id={"grid": target}, device_id_type=MESH)

    @pl.when(has_left)
    def _():
        greet(left)

    @pl.when(has_right)
    def _():
        greet(right)

    if Y > 1:
        greet(partner)
    greet(sibling)
    pl.semaphore_wait(
        barrier, (2 if Y > 1 else 1) + has_left.astype(jnp.int32) + has_right.astype(jnp.int32)
    )

    def remote(src, dst, send, got, target):
        return pltpu.make_async_remote_copy(
            src_ref=src, dst_ref=dst, send_sem=send, recv_sem=got,
            device_id={"grid": target}, device_id_type=MESH,
        )

    def own(p):
        half = K // 2
        ref = s_ref if p < half else t_ref
        return ref.at[pl.ds((p % half) * R, R), :]

    order = list(range(PA, K)) + list(range(PA))
    if Y > 1:
        for p in order:
            remote(own(p), g.at[me, pl.ds(p * R, R), :], ysend.at[z], recv.at[z * Y + y, p], partner).start()

    @pl.when(has_right)
    def _():
        for p in range(K):
            remote(own(p), g.at[me, pl.ds(p * R, R), :], zsend.at[0, z], recv.at[z * Y + y, p], right).start()

    @pl.when(has_left)
    def _():
        for p in range(K):
            remote(own(p), g.at[me, pl.ds(p * R, R), :], zsend.at[1, z], recv.at[z * Y + y, p], left).start()

    locals_ = []
    for h, ref in enumerate((s_ref, t_ref)):
        dst = g.at[me, pl.ds(h * tokens, tokens), :]
        remote(ref, dst, csend.at[z * Y + y], crecv.at[z * Y + y, h], sibling).start()
        cp = pltpu.make_async_copy(ref, dst, local_sem.at[h])
        cp.start()
        locals_.append(cp)

    def wait_piece(zz, yy, p):
        at = g.at[dev(zz, yy, c), rows(p), :]
        remote(at, at, csend.at[zz * Y + yy], recv.at[zz * Y + yy, p], sibling).wait_recv()

    def send_piece(zz, yy, p, send, target):
        at = g.at[dev(zz, yy, c), rows(p), :]
        remote(at, at, send, recv.at[zz * Y + yy, p], target).start()

    def share_piece(zz, yy, p):
        at = g.at[dev(zz, yy, c), rows(p), :]
        half = jnp.int32(p >= K // 2)
        remote(at, at, csend.at[zz * Y + yy], crecv.at[zz * Y + yy, half], sibling).start()

    for cp in locals_:
        cp.wait()
    st[...] = g[me, pl.ds(0, tokens), :].T

    def multiply(zz, yy, first, count):
        @pl.loop(first, first + count)
        def _(kind):
            half, other = kind // 2, kind % 2
            block = dev(zz, yy, jnp.where(other == 1, 1 - c, c))
            at = g.at[block, pl.ds(pl.multiple_of(half * tokens, tokens), tokens), :]

            @pl.when(other == 1)
            def _():
                remote(at, at, csend.at[0], crecv.at[zz * Y + yy, half], sibling).wait_recv()

            out[half, :, pl.ds(pl.multiple_of(block * width, width), width)] = (
                jnp.dot(st[...], at[...], preferred_element_type=jnp.float32) * (1.0 / tokens)
            )

    per = K + (PB if Y > 1 else 0)

    def picks(q, table):
        first, count = jnp.int32(0), jnp.int32(0)
        for when, a, b in table:
            first, count = jnp.where(q == when, a, first), jnp.where(q == when, b, count)
        return first, count

    if Y > 1:
        z_table = ((K // 2, 0, 1), (K // 2 + 2, 1, 1), (K, 2, 1), (per - 1, 3, 1))
    else:
        z_table = ((K // 2, 0, 1), (K - 1, 1, 3))
    y_table = ((K // 2, 0, 1), (K // 2 + 2, 1, 1), (PA - 1, 2, 2))
    n_left, n_right = z, Z - 1 - z
    least = jnp.minimum(n_left, n_right)

    def from_z(t, side):
        k = t // per + 1
        q = t % per
        zo = z - k if side == 0 else z + k
        there = zo >= 0 if side == 0 else zo <= Z - 1
        onward = has_right if side == 0 else has_left
        target = right if side == 0 else left

        @pl.when(there & (q < K))
        def _():
            wait_piece(zo, y, q)

            @pl.when(onward)
            def _():
                send_piece(zo, y, q, zsend.at[side, zo], target)

            if Y > 1:
                @pl.when(q < PA)
                def _():
                    send_piece(zo, y, q, ysend.at[zo], partner)

            share_piece(zo, y, q)

        if Y > 1 and PB > 0:
            @pl.when(there & (q >= K))
            def _():
                yo, p = Y - 1 - y, q - PB
                wait_piece(zo, yo, p)

                @pl.when(onward)
                def _():
                    send_piece(zo, yo, p, zsendp.at[side, zo], target)

                share_piece(zo, yo, p)

        first, count = picks(q, z_table)
        return zo, y, first, jnp.where(there, count, 0)

    def from_y(u):
        yo = Y - 1 - y

        @pl.when(u < PB)
        def _():
            p = PA + u
            wait_piece(z, yo, p)

            @pl.when(has_right)
            def _():
                send_piece(z, yo, p, zsendp.at[0, z], right)

            @pl.when(has_left)
            def _():
                send_piece(z, yo, p, zsendp.at[1, z], left)

            share_piece(z, yo, p)

        i = u - K
        both = i < 2 * PA * least
        i1 = i - 2 * PA * least
        pair = i // 2
        k = jnp.where(both, pair // PA, least + i1 // PA) + 1
        go_left = jnp.where(both, i % 2, (n_left < n_right).astype(jnp.int32))
        far = jnp.where(go_left == 1, z + k, z - k)
        direct = u < K
        zo = jnp.where(direct, z, far)
        p = jnp.where(direct, u - PB, jnp.where(both, pair % PA, i1 % PA))

        @pl.when((u >= PB) & (u < y_slots))
        def _():
            wait_piece(zo, yo, p)
            share_piece(zo, yo, p)

        first, count = picks(p, y_table)
        return zo, yo, first, jnp.where((u >= PB) & (u < y_slots), count, 0)

    slots = per * (Z - 1)
    y_slots = K + PA * (Z - 1) if Y > 1 else 0

    multiply(z, y, 0, 4)

    @pl.loop(0, max(slots, y_slots))
    def _(t):
        work = [from_z(t, 0), from_z(t, 1)]
        if y_slots:
            work.append(from_y(t))
        for todo in work:
            multiply(*todo)

    @pl.loop(0, Z)
    def _(zo):
        for side in range(2):
            sent = (zo <= z) & has_right if side == 0 else (zo >= z) & has_left

            @pl.when(sent)
            def _():
                at = g.at[0]
                remote(at, at, zsend.at[side, zo], crecv.at[0, 0], sibling).wait_send()
                if Y > 1 and PB > 0:
                    at = g.at[0, pl.ds(PA * R, PB * R), :]
                    remote(at, at, zsendp.at[side, zo], crecv.at[0, 0], sibling).wait_send()

        if Y > 1:
            @pl.when(zo == z)
            def _():
                at = g.at[0]
                remote(at, at, ysend.at[zo], crecv.at[0, 0], sibling).wait_send()

            @pl.when(zo != z)
            def _():
                at = g.at[0, pl.ds(0, PA * R), :]
                remote(at, at, ysend.at[zo], crecv.at[0, 0], sibling).wait_send()

        for yo in range(Y):
            at = g.at[0]
            remote(at, at, csend.at[zo * Y + yo], crecv.at[0, 0], sibling).wait_send()


def gather_products(source, target, Z, Y):
    tokens, width = source.shape
    PA, PB = (10, 2) if Y > 1 else (4, 0)
    n = Z * Y * 2
    dma = pltpu.SemaphoreType.DMA
    return pl.pallas_call(
        functools.partial(gather_kernel, Z, Y, PA, PB),
        out_shape=pltpu.VMEM((2, width, n * width), jnp.float32),
        in_specs=[pl.BlockSpec(memory_space=pl.ANY)] * 2,
        out_specs=pl.BlockSpec(memory_space=pltpu.VMEM),
        scratch_shapes=[
            pltpu.VMEM((n, 2 * tokens, width), source.dtype),
            pltpu.VMEM((width, tokens), source.dtype),
            dma((2,)),
            dma((Z * Y, PA + PB)),
            dma((Z * Y, 2)),
            dma((2, Z)),
            dma((2, Z)),
            dma((Z,)),
            dma((Z * Y,)),
        ],
        compiler_params=pltpu.CompilerParams(
            collective_id=0, has_side_effects=True, vmem_limit_bytes=28 << 20
        ),
        cost_estimate=pl.CostEstimate(
            flops=4 * width * width * n * tokens,
            bytes_accessed=n * width * (4 * tokens + 8 * width),
            transcendentals=0,
        ),
    )(source, target)


def store_kernel(products, cross_ref, self_ref, sem):
    width = products.shape[1]
    parts = sem.shape[1]
    rows = width // parts
    copies = []
    for part in range(parts):
        at = pl.ds(part * rows, rows)
        for half, ref in enumerate((self_ref, cross_ref)):
            copies.append(
                pltpu.make_async_copy(products.at[half, at, :], ref.at[at, :], sem.at[half, part])
            )
            copies[-1].start()
    for copy in copies:
        copy.wait()


def store(products):
    _, width, columns = products.shape
    out = jax.ShapeDtypeStruct((width, columns), jnp.float32)
    return pl.pallas_call(
        store_kernel,
        out_shape=(out, out),
        in_specs=[pl.BlockSpec(memory_space=pl.ANY)],
        out_specs=(pl.BlockSpec(memory_space=pl.ANY),) * 2,
        scratch_shapes=[pltpu.SemaphoreType.DMA((2, 8))],
        compiler_params=pltpu.CompilerParams(vmem_limit_bytes=1 << 20),
        cost_estimate=pl.CostEstimate(
            flops=0, bytes_accessed=8 * width * columns, transcendentals=0
        ),
    )(pltpu.with_memory_space_constraint(products, pltpu.VMEM))


def solution(mesh):
    n = mesh.shape["grid"]
    Y = max(1, 4 // mesh.shape["groups"])
    Z = n // (2 * Y)

    def shards(source, target):
        return store(gather_products(source, target, Z, Y))

    specs = (P("groups", "grid"), P("groups", "grid"))
    out_specs = (P(("groups", "grid"), None), P(("groups", "grid"), None))
    return jax.shard_map(shards, mesh=mesh, in_specs=specs, out_specs=out_specs, check_vma=False)
```

```python
import functools

import jax
import jax.numpy as jnp
from jax import lax
from jax.experimental import pallas as pl
from jax.experimental.pallas import tpu as pltpu
from jax.sharding import PartitionSpec as P

MESH = pl.DeviceIdType.MESH


def gather_kernel(Z, Y, PA, PB, s_ref, t_ref, out, g, st, local_sem, recv, crecv, zsend, zsendp, ysend, csend):
    K = PA + PB
    tokens, width = s_ref.shape
    R = 2 * tokens // K
    me = lax.axis_index("grid")
    c = me % 2
    y = (me // 2) % Y
    z = me // (2 * Y)

    def dev(zz, yy, cc):
        return (zz * Y + yy) * 2 + cc

    def rows(p):
        return pl.ds(pl.multiple_of(p * R, R), R)

    left, right = dev(z - 1, y, c), dev(z + 1, y, c)
    partner, sibling = dev(z, Y - 1 - y, c), dev(z, y, 1 - c)
    has_left, has_right = z > 0, z < Z - 1

    barrier = pltpu.get_barrier_semaphore()

    def greet(target):
        pl.semaphore_signal(barrier, inc=1, device_id={"grid": target}, device_id_type=MESH)

    @pl.when(has_left)
    def _():
        greet(left)

    @pl.when(has_right)
    def _():
        greet(right)

    if Y > 1:
        greet(partner)
    greet(sibling)
    pl.semaphore_wait(
        barrier, (2 if Y > 1 else 1) + has_left.astype(jnp.int32) + has_right.astype(jnp.int32)
    )

    def remote(src, dst, send, got, target):
        return pltpu.make_async_remote_copy(
            src_ref=src, dst_ref=dst, send_sem=send, recv_sem=got,
            device_id={"grid": target}, device_id_type=MESH,
        )

    def own(p):
        half = K // 2
        ref = s_ref if p < half else t_ref
        return ref.at[pl.ds((p % half) * R, R), :]

    order = list(range(PA, K)) + list(range(PA))
    @pl.when(has_right)
    def _():
        for p in range(K):
            remote(own(p), g.at[me, pl.ds(p * R, R), :], zsend.at[0, z], recv.at[z * Y + y, p], right).start()

    @pl.when(has_left)
    def _():
        for p in range(K):
            remote(own(p), g.at[me, pl.ds(p * R, R), :], zsend.at[1, z], recv.at[z * Y + y, p], left).start()

    if Y > 1:
        for p in order:
            remote(own(p), g.at[me, pl.ds(p * R, R), :], ysend.at[z], recv.at[z * Y + y, p], partner).start()

    locals_ = []
    for h, ref in enumerate((s_ref, t_ref)):
        dst = g.at[me, pl.ds(h * tokens, tokens), :]
        remote(ref, dst, csend.at[z * Y + y], crecv.at[z * Y + y, h], sibling).start()
        cp = pltpu.make_async_copy(ref, dst, local_sem.at[h])
        cp.start()
        locals_.append(cp)

    def wait_piece(zz, yy, p):
        at = g.at[dev(zz, yy, c), rows(p), :]
        remote(at, at, csend.at[zz * Y + yy], recv.at[zz * Y + yy, p], sibling).wait_recv()

    def send_piece(zz, yy, p, send, target):
        at = g.at[dev(zz, yy, c), rows(p), :]
        remote(at, at, send, recv.at[zz * Y + yy, p], target).start()

    def share_piece(zz, yy, p):
        at = g.at[dev(zz, yy, c), rows(p), :]
        half = jnp.int32(p >= K // 2)
        remote(at, at, csend.at[zz * Y + yy], crecv.at[zz * Y + yy, half], sibling).start()

    for cp in locals_:
        cp.wait()
    st[...] = g[me, pl.ds(0, tokens), :].T

    def multiply(zz, yy, first, count):
        @pl.loop(first, first + count)
        def _(kind):
            half, other = kind // 2, kind % 2
            block = dev(zz, yy, jnp.where(other == 1, 1 - c, c))
            at = g.at[block, pl.ds(pl.multiple_of(half * tokens, tokens), tokens), :]

            @pl.when(other == 1)
            def _():
                remote(at, at, csend.at[0], crecv.at[zz * Y + yy, half], sibling).wait_recv()

            out[half, :, pl.ds(pl.multiple_of(block * width, width), width)] = (
                jnp.dot(st[...], at[...], preferred_element_type=jnp.float32) * (1.0 / tokens)
            )

    per = K + (PB if Y > 1 else 0)

    def picks(q, table):
        first, count = jnp.int32(0), jnp.int32(0)
        for when, a, b in table:
            first, count = jnp.where(q == when, a, first), jnp.where(q == when, b, count)
        return first, count

    if Y > 1:
        z_table = ((K // 2, 0, 1), (K // 2 + 2, 1, 1), (K, 2, 1), (per - 1, 3, 1))
    else:
        z_table = ((K // 2, 0, 1), (K - 1, 1, 3))
    y_table = ((K // 2, 0, 1), (K // 2 + 2, 1, 1), (PA - 1, 2, 2))
    n_left, n_right = z, Z - 1 - z
    least = jnp.minimum(n_left, n_right)

    def from_z(t, side):
        k = t // per + 1
        q = t % per
        zo = z - k if side == 0 else z + k
        there = zo >= 0 if side == 0 else zo <= Z - 1
        onward = has_right if side == 0 else has_left
        target = right if side == 0 else left

        @pl.when(there & (q < K))
        def _():
            wait_piece(zo, y, q)

            @pl.when(onward)
            def _():
                send_piece(zo, y, q, zsend.at[side, zo], target)

            if Y > 1:
                @pl.when(q < PA)
                def _():
                    send_piece(zo, y, q, ysend.at[zo], partner)

            share_piece(zo, y, q)

        if Y > 1 and PB > 0:
            @pl.when(there & (q >= K))
            def _():
                yo, p = Y - 1 - y, q - PB
                wait_piece(zo, yo, p)

                @pl.when(onward)
                def _():
                    send_piece(zo, yo, p, zsendp.at[side, zo], target)

                share_piece(zo, yo, p)

        first, count = picks(q, z_table)
        return zo, y, first, jnp.where(there, count, 0)

    def from_y(u):
        yo = Y - 1 - y

        @pl.when(u < PB)
        def _():
            p = PA + u
            wait_piece(z, yo, p)

            @pl.when(has_right)
            def _():
                send_piece(z, yo, p, zsendp.at[0, z], right)

            @pl.when(has_left)
            def _():
                send_piece(z, yo, p, zsendp.at[1, z], left)

            share_piece(z, yo, p)

        i = u - K
        both = i < 2 * PA * least
        i1 = i - 2 * PA * least
        pair = i // 2
        k = jnp.where(both, pair // PA, least + i1 // PA) + 1
        go_left = jnp.where(both, i % 2, (n_left < n_right).astype(jnp.int32))
        far = jnp.where(go_left == 1, z + k, z - k)
        direct = u < K
        zo = jnp.where(direct, z, far)
        p = jnp.where(direct, u - PB, jnp.where(both, pair % PA, i1 % PA))

        @pl.when((u >= PB) & (u < y_slots))
        def _():
            wait_piece(zo, yo, p)
            share_piece(zo, yo, p)

        first, count = picks(p, y_table)
        return zo, yo, first, jnp.where((u >= PB) & (u < y_slots), count, 0)

    slots = per * (Z - 1)
    y_slots = K + PA * (Z - 1) if Y > 1 else 0

    multiply(z, y, 0, 4)

    @pl.loop(0, max(slots, y_slots))
    def _(t):
        work = [from_z(t, 0), from_z(t, 1)]
        if y_slots:
            work.append(from_y(t))
        for todo in work:
            multiply(*todo)

    @pl.loop(0, Z)
    def _(zo):
        for side in range(2):
            sent = (zo <= z) & has_right if side == 0 else (zo >= z) & has_left

            @pl.when(sent)
            def _():
                at = g.at[0]
                remote(at, at, zsend.at[side, zo], crecv.at[0, 0], sibling).wait_send()
                if Y > 1 and PB > 0:
                    at = g.at[0, pl.ds(PA * R, PB * R), :]
                    remote(at, at, zsendp.at[side, zo], crecv.at[0, 0], sibling).wait_send()

        if Y > 1:
            @pl.when(zo == z)
            def _():
                at = g.at[0]
                remote(at, at, ysend.at[zo], crecv.at[0, 0], sibling).wait_send()

            @pl.when(zo != z)
            def _():
                at = g.at[0, pl.ds(0, PA * R), :]
                remote(at, at, ysend.at[zo], crecv.at[0, 0], sibling).wait_send()

        for yo in range(Y):
            at = g.at[0]
            remote(at, at, csend.at[zo * Y + yo], crecv.at[0, 0], sibling).wait_send()


def gather_products(source, target, Z, Y):
    tokens, width = source.shape
    PA, PB = (10, 2) if Y > 1 else (4, 0)
    n = Z * Y * 2
    dma = pltpu.SemaphoreType.DMA
    return pl.pallas_call(
        functools.partial(gather_kernel, Z, Y, PA, PB),
        out_shape=pltpu.VMEM((2, width, n * width), jnp.float32),
        in_specs=[pl.BlockSpec(memory_space=pl.ANY)] * 2,
        out_specs=pl.BlockSpec(memory_space=pltpu.VMEM),
        scratch_shapes=[
            pltpu.VMEM((n, 2 * tokens, width), source.dtype),
            pltpu.VMEM((width, tokens), source.dtype),
            dma((2,)),
            dma((Z * Y, PA + PB)),
            dma((Z * Y, 2)),
            dma((2, Z)),
            dma((2, Z)),
            dma((Z,)),
            dma((Z * Y,)),
        ],
        compiler_params=pltpu.CompilerParams(
            collective_id=0, has_side_effects=True, vmem_limit_bytes=28 << 20
        ),
        cost_estimate=pl.CostEstimate(
            flops=4 * width * width * n * tokens,
            bytes_accessed=n * width * (4 * tokens + 8 * width),
            transcendentals=0,
        ),
    )(source, target)


def store_kernel(products, cross_ref, self_ref, sem):
    width = products.shape[1]
    parts = sem.shape[1]
    rows = width // parts
    copies = []
    for part in range(parts):
        at = pl.ds(part * rows, rows)
        for half, ref in enumerate((self_ref, cross_ref)):
            copies.append(
                pltpu.make_async_copy(products.at[half, at, :], ref.at[at, :], sem.at[half, part])
            )
            copies[-1].start()
    for copy in copies:
        copy.wait()


def store(products):
    _, width, columns = products.shape
    out = jax.ShapeDtypeStruct((width, columns), jnp.float32)
    return pl.pallas_call(
        store_kernel,
        out_shape=(out, out),
        in_specs=[pl.BlockSpec(memory_space=pl.ANY)],
        out_specs=(pl.BlockSpec(memory_space=pl.ANY),) * 2,
        scratch_shapes=[pltpu.SemaphoreType.DMA((2, 8))],
        compiler_params=pltpu.CompilerParams(vmem_limit_bytes=1 << 20),
        cost_estimate=pl.CostEstimate(
            flops=0, bytes_accessed=8 * width * columns, transcendentals=0
        ),
    )(pltpu.with_memory_space_constraint(products, pltpu.VMEM))


def solution(mesh):
    n = mesh.shape["grid"]
    Y = max(1, 4 // mesh.shape["groups"])
    Z = n // (2 * Y)

    def shards(source, target):
        return store(gather_products(source, target, Z, Y))

    specs = (P("groups", "grid"), P("groups", "grid"))
    out_specs = (P(("groups", "grid"), None), P(("groups", "grid"), None))
    return jax.shard_map(shards, mesh=mesh, in_specs=specs, out_specs=out_specs, check_vma=False)
```
